32 devices in a mesh: grp: 2 (over x), dp: 16 (over z, y, core).
Axes of the slice: x: 2, y: 2, z: 4, core: 2. Of those that a mesh axis runs over, the one named last changes fastest.
Arguments:
- start_state: bfloat16 [4096, 512], P(('grp', 'dp')), may hold values from -6 to 6
- w_up: bfloat16 [512, 1024], replicated, may hold values from -0.25 to 0.25
- b_up: float32 [1024], replicated, may hold values from -3 to 3
- w_down: bfloat16 [1024, 512], replicated, may hold values from -0.1875 to 0.1875
- w_spread: bfloat16 [512, 1024], replicated, may hold values from -0.25 to 0.25
- w_scale: bfloat16 [1024, 512], replicated, may hold values from -0.1875 to 0.1875
- b_scale: float32 [512], replicated, may hold values from -4 to 4
- brownian_noise: bfloat16 [3, 4096, 512], P(None, ('grp', 'dp')), may hold values from -5 to 5
- step_mults: int32 [3, 4096], P(None, ('grp', 'dp')), may hold values from 1 to 4
- accept_flags: int32 [3, 4096], P(None, ('grp', 'dp')), may hold values 0 or 1
- cotangent: bfloat16 [4096, 512], P(('grp', 'dp')), may hold values from -6 to 6
Outputs:
- err_norms: float32 [3], replicated
- grad_up: float32 [512, 1024], P('dp')
- grad_down: float32 [512, 1024], P('dp')
The draws below stay inside these ranges and needn't reach their ends.
All inputs are finite; a program needn't handle non-finite values. No bound on the sum of `accept_flags` on one device may be relied on, other than what follows from the above.
Results may differ from the reference program's by a relative error of at most 0.0033.
Values sent between devices are 32-bit elements; how exact they have to be, the bound alone decides.
A program may use at most 64 MiB of HBM per device.

```python
import jax
import jax.numpy as jnp
from jax import lax

LATENT = 512
HIDDEN_SIZE = 1024
STEPS = 3
SEQ = 4096


def set_ends(result, stream_key, low, largest):
    place = [jax.random.randint(jax.random.fold_in(stream_key, axis), (), 0, length) for axis, length in enumerate(result.shape)]
    widest = result.shape.index(max(result.shape))
    neighbour = place[:widest] + [(place[widest] + 1) % result.shape[widest]] + place[widest + 1:]
    return result.at[tuple(place)].set(low).at[tuple(neighbour)].set(largest)


def strengthened(drawn, key, source, target, parts, factor):
    owner, partner = [(jnp.arange(drawn.shape[dim]) // (drawn.shape[dim] // parts)).reshape([-1 if axis == dim else 1 for axis in range(drawn.ndim)]) for dim in (source, target)]
    chosen = jax.random.permutation(key, parts)[partner]
    strong = (owner == chosen) | (owner == (partner + parts // 2) % parts)
    return jnp.where(strong, factor * drawn, drawn)


def block_scale(rng, extent, split, least, top_value):
    gain = 1.0
    for position, parts in split:
        steps = jax.random.uniform(jax.random.fold_in(jax.random.fold_in(rng, 6), position), (parts,), jnp.float32, least / len(split), top_value / len(split))
        gain = gain * jnp.repeat(jnp.exp(steps), extent[position] // parts).reshape((-1,) + (1,) * (len(extent) - 1 - position))
    return gain


def normal_values(rng, dims, deviation, reach, split=(), held_as=jnp.bfloat16):
    drawn = jax.random.normal(rng, dims, jnp.float32) * deviation
    if len(split) > 0:
        drawn = block_scale(rng, dims, split, -0.22, 0.18) * drawn
    return jnp.clip(drawn, min=-reach, max=reach).astype(held_as)


def heavy_noise(rng, extent, scale, most, cuts, heavy, dtype=jnp.bfloat16):
    array = scale * jax.random.normal(rng, extent, jnp.float32)
    if cuts:
        array = array * block_scale(rng, extent, cuts, -0.22, 0.18)
    return jnp.clip(strengthened(array, jax.random.fold_in(rng, 3), *heavy), -most, most).astype(dtype)


def setup_inputs(seed: int = 0) -> dict:
    key_list = jax.random.split(jax.random.key(seed), 12)
    start_state = heavy_noise(key_list[0], (SEQ, LATENT), 1.0, 6.0, ((0, 32),), (0, 1, 32, 2.75))
    w_up = normal_values(key_list[1], (LATENT, HIDDEN_SIZE), LATENT ** -0.5, 0.25)
    b_up = normal_values(key_list[2], (HIDDEN_SIZE,), 0.5, 3.0, (), jnp.float32)
    w_down = normal_values(key_list[3], (HIDDEN_SIZE, LATENT), HIDDEN_SIZE ** -0.5, 0.1875)
    w_spread = normal_values(key_list[4], (LATENT, HIDDEN_SIZE), LATENT ** -0.5, 0.25)
    w_scale = normal_values(key_list[5], (HIDDEN_SIZE, LATENT), HIDDEN_SIZE ** -0.5, 0.1875)
    b_scale = normal_values(key_list[6], (LATENT,), 1.0, 4.0, (), jnp.float32)
    brownian_noise = normal_values(key_list[7], (STEPS, SEQ, LATENT), 1.0, 5.0, ((1, 32),))
    step_mults = set_ends(jax.random.randint(key_list[8], (STEPS, SEQ), 1, 5), jax.random.fold_in(key_list[8], 1), 1, 4).astype(jnp.int32)
    accept_flags = set_ends((jax.random.randint(key_list[9], (STEPS, SEQ), 0, 4) < 3).astype(jnp.int32), jax.random.fold_in(key_list[9], 1), 0, 1)
    cotangent = normal_values(key_list[10], (SEQ, LATENT), 1.0, 6.0, ((0, 32),))
    return dict(start_state=start_state, w_up=w_up, b_up=b_up, w_down=w_down, w_spread=w_spread, w_scale=w_scale, b_scale=b_scale, brownian_noise=brownian_noise, step_mults=step_mults, accept_flags=accept_flags, cotangent=cotangent)


base_step = 0.05
abs_tol = 0.01
rel_tol = 0.01

def diffuse(current, w_first, w_second, b_second):
    inner = jax.nn.silu(jnp.dot(current.astype(jnp.bfloat16), w_first, preferred_element_type=jnp.float32))
    outer = jnp.dot(inner.astype(jnp.bfloat16), w_second, preferred_element_type=jnp.float32)
    return 0.6 * jax.nn.sigmoid(outer + b_second)

def forward_step(current, w_up, b_up, w_down, w_spread, w_scale, b_scale, noise_now, mult_now, flag_now):
    low_state = current.astype(jnp.bfloat16)
    pre_act = jnp.dot(low_state, w_up, preferred_element_type=jnp.float32) + b_up
    hidden = jax.nn.silu(pre_act).astype(jnp.bfloat16)
    drift_out = jnp.dot(hidden, w_down, preferred_element_type=jnp.float32)
    step_size = mult_now.astype(jnp.float32)[:, None] * base_step
    sqrt_step = jnp.sqrt(step_size)
    brownian = sqrt_step * noise_now.astype(jnp.float32)
    keep_mask = flag_now.astype(jnp.float32)[:, None]

    def update(before):
        spread = diffuse(before, w_spread, w_scale, b_scale)
        shifted = diffuse(before + spread * sqrt_step, w_spread, w_scale, b_scale)
        milstein = (shifted - spread) * (brownian * brownian - step_size) / (2.0 * sqrt_step)
        proposal = before + drift_out * step_size + spread * brownian + milstein
        return (keep_mask * proposal + (1.0 - keep_mask) * before, milstein)
    (advanced, milstein), pull_back = jax.vjp(update, current)
    scaled = milstein / (abs_tol + rel_tol * jnp.abs(current))
    err_part = jnp.sum(scaled * scaled)
    return (advanced, err_part, (low_state, pre_act, hidden, pull_back, step_size, keep_mask))

def backward_step(cot_state, record, w_up, w_down, grad_up, grad_down):
    low_state, pre_act, hidden, pull_back, step_size, keep_mask = record
    cot_drift = (cot_state * keep_mask * step_size).astype(jnp.bfloat16)
    grad_down = grad_down + lax.dot_general(cot_drift, hidden, (((0,), (0,)), ((), ())), preferred_element_type=jnp.float32)
    sigma = jax.nn.sigmoid(pre_act)
    back_pre = lax.dot_general(cot_drift, w_down, (((1,), (1,)), ((), ())), preferred_element_type=jnp.float32)
    cot_pre = (back_pre * sigma * (1.0 + pre_act * (1.0 - sigma))).astype(jnp.bfloat16)
    grad_up = grad_up + lax.dot_general(low_state, cot_pre, (((0,), (0,)), ((), ())), preferred_element_type=jnp.float32)
    through = pull_back((cot_state, jnp.zeros_like(cot_state)))[0]
    cot_state = through + lax.dot_general(cot_pre, w_up, (((1,), (1,)), ((), ())), preferred_element_type=jnp.float32)
    return (cot_state, grad_up, grad_down)

def reference(start_state, w_up, b_up, w_down, w_spread, w_scale, b_scale, brownian_noise, step_mults, accept_flags, cotangent):
    current = start_state.astype(jnp.float32)
    records = []
    err_sums = []
    for step_index in range(STEPS):
        current, err_part, record = forward_step(current, w_up, b_up, w_down, w_spread, w_scale, b_scale, brownian_noise[step_index], step_mults[step_index], accept_flags[step_index])
        records.append(record)
        err_sums.append(err_part)
    err_norms = jnp.sqrt(jnp.stack(err_sums) / (SEQ * LATENT))
    cot_state = cotangent.astype(jnp.float32)
    grad_up = jnp.zeros((LATENT, HIDDEN_SIZE), jnp.float32)
    grad_down = jnp.zeros((LATENT, HIDDEN_SIZE), jnp.float32)
    for step_index in reversed(range(STEPS)):
        cot_state, grad_up, grad_down = backward_step(cot_state, records[step_index], w_up, w_down, grad_up, grad_down)
    return (err_norms, grad_up, grad_down)
```

```python
import functools

import jax
import jax.numpy as jnp
from jax import lax
from jax.experimental import pallas as pl
from jax.experimental.pallas import tpu as pltpu
from jax.sharding import PartitionSpec as P

base_step = 0.05
abs_tol = 0.01
rel_tol = 0.01
cores = 2
inner = 2
MESH = pl.DeviceIdType.MESH
f32 = jnp.float32
bf16 = jnp.bfloat16


def sigmoid(x):
    return 0.5 * jnp.tanh(0.5 * x) + 0.5


def dot(a, b):
    return jnp.dot(a, b, preferred_element_type=f32)


def dot_t(a, b):
    return lax.dot_general(a, b, (((1,), (1,)), ((), ())), preferred_element_type=f32)


def blocks(extent, width=256):
    width = min(width, extent)
    return [slice(at, at + width) for at in range(0, extent, width)]


def silu_pair(x):
    s = sigmoid(x)
    y = x * s
    return y.astype(bf16), s + y * (1.0 - s)


def prepare(ins, work):
    steps, rows = ins["mults"].shape
    table = work["table"]
    table[...] = jnp.zeros_like(table)
    table[0:steps, :] = ins["mults"][...].astype(f32) * base_step
    table[steps : 2 * steps, :] = ins["flags"][...].astype(f32)
    turned = table[...].T
    lanes = table.shape[0]
    for n in range(steps):
        h = jnp.broadcast_to(turned[:, n : n + 1], (rows, lanes))
        work["h"][n] = h
        work["r"][n] = jnp.sqrt(h)
        work["keep"][n] = jnp.broadcast_to(turned[:, steps + n : steps + n + 1], (rows, lanes))
    work["cur"][...] = ins["start"][...].astype(f32)
    work["cot"][...] = ins["cot"][...].astype(f32)
    work["err"][...] = jnp.zeros_like(work["err"])


def forward(n, ins, work):
    rows, latent = work["cur"].shape
    hidden = ins["w_up"].shape[1]
    at = pl.ds(pl.multiple_of(n * rows, rows), rows)
    h = work["h"][n][:, 0:1]
    r = work["r"][n][:, 0:1]
    keep = work["keep"][n][:, 0:1]
    cur = work["cur"][...]
    low = cur.astype(bf16)
    work["low_t"][:, at] = cur.T.astype(bf16)
    for j in blocks(hidden):
        work["in1"][:, j], work["d_in1"][n, :, j] = silu_pair(dot(low, ins["w_spread"][:, j]))
    for j in blocks(hidden):
        x = dot(low, ins["w_up"][:, j]) + ins["b_up"][:, j]
        work["hid"][at, j], work["d_hid"][n, :, j] = silu_pair(x)
    for j in blocks(latent):
        s = sigmoid(dot(work["in1"][...], ins["w_scale"][:, j]) + ins["b_scale"][:, j])
        g = 0.6 * s
        work["g"][:, j] = g
        work["d_g1"][n, :, j] = g * (1.0 - s)
        work["low2"][:, j] = (work["cur"][:, j] + g * r).astype(bf16)
    for j in blocks(hidden):
        work["in2"][:, j], work["d_in2"][n, :, j] = silu_pair(
            dot(work["low2"][...], ins["w_spread"][:, j])
        )
    total = jnp.zeros((1, 128), f32)
    for j in blocks(latent):
        s = sigmoid(dot(work["in2"][...], ins["w_scale"][:, j]) + ins["b_scale"][:, j])
        gbar = 0.6 * s
        work["d_g2"][n, :, j] = gbar * (1.0 - s)
        drift = dot(work["hid"][at, :], ins["w_down"][:, j])
        noise = ins["noise"][n, :, j].astype(f32)
        g = work["g"][:, j]
        c = work["cur"][:, j]
        milstein = (gbar - g) * (0.5 * r * (noise * noise - 1.0))
        scaled = milstein / (abs_tol + rel_tol * jnp.abs(c))
        part = jnp.sum(scaled * scaled, axis=0, keepdims=True)
        for i in blocks(part.shape[1], 128):
            total = total + part[:, i]
        proposal = c + drift * h + g * (r * noise) + milstein
        work["cur"][:, j] = jnp.where(keep > 0.5, proposal, c)
    work["err"][pl.ds(n, 1), :] = total


def back_drift(n, ins, work):
    rows, latent = work["cur"].shape
    at = pl.ds(pl.multiple_of(n * rows, rows), rows)
    cd = work["cot"][...] * (work["keep"][n][:, 0:1] * work["h"][n][:, 0:1])
    work["cd"][...] = cd.astype(bf16)
    work["cd_t"][:, at] = cd.T.astype(bf16)


def back_pre(n, ins, work):
    rows, latent = work["cur"].shape
    hidden = ins["w_up"].shape[1]
    at = pl.ds(pl.multiple_of(n * rows, rows), rows)
    for j in blocks(hidden):
        back = dot_t(work["cd"][...], ins["w_down"][j, :])
        work["cpre"][at, j] = (back * work["d_hid"][n, :, j]).astype(bf16)


def back_state(n, ins, work):
    rows, latent = work["cur"].shape
    hidden = ins["w_up"].shape[1]
    at = pl.ds(pl.multiple_of(n * rows, rows), rows)
    r = work["r"][n][:, 0:1]
    keep = work["keep"][n][:, 0:1]
    for j in blocks(latent):
        noise = ins["noise"][n, :, j].astype(f32)
        ck = keep * work["cot"][:, j]
        to_bar = ck * (0.5 * r * (noise * noise - 1.0))
        work["to_g"][:, j] = ck * (r * noise) - to_bar
        work["d_out"][:, j] = (to_bar * work["d_g2"][n, :, j]).astype(bf16)
    for j in blocks(hidden):
        back = dot_t(work["d_out"][...], ins["w_scale"][j, :]).astype(bf16).astype(f32)
        work["in2"][:, j] = (back * work["d_in2"][n, :, j]).astype(bf16)
    for j in blocks(latent):
        back = dot_t(work["in2"][...], ins["w_spread"][j, :]).astype(bf16).astype(f32)
        work["g"][:, j] = back
        work["d_out"][:, j] = (
            (work["to_g"][:, j] + back * r) * work["d_g1"][n, :, j]
        ).astype(bf16)
    for j in blocks(hidden):
        back = dot_t(work["d_out"][...], ins["w_scale"][j, :]).astype(bf16).astype(f32)
        work["in1"][:, j] = (back * work["d_in1"][n, :, j]).astype(bf16)
    for j in blocks(latent):
        back = dot_t(work["in1"][...], ins["w_spread"][j, :]).astype(bf16).astype(f32)
        through = dot_t(work["cpre"][at, :], ins["w_up"][j, :])
        work["cot"][:, j] = work["cot"][:, j] + work["g"][:, j] + back + through


names = (
    "start", "w_up", "b_up", "w_down", "w_spread", "w_scale", "b_scale", "noise", "mults",
    "flags", "cot",
)


def work_shapes(steps, rows, latent, hidden):
    vm = pltpu.VMEM
    return dict(
        table=vm((128, rows), f32),
        h=vm((steps, rows, 128), f32),
        r=vm((steps, rows, 128), f32),
        keep=vm((steps, rows, 128), f32),
        cur=vm((rows, latent), f32),
        cot=vm((rows, latent), f32),
        err=vm((8, 128), f32),
        low_t=vm((latent, steps * rows), bf16),
        cd_t=vm((latent, steps * rows), bf16),
        hid=vm((steps * rows, hidden), bf16),
        cpre=vm((steps * rows, hidden), bf16),
        d_hid=vm((steps, rows, hidden), f32),
        in1=vm((rows, hidden), bf16),
        d_in1=vm((steps, rows, hidden), f32),
        in2=vm((rows, hidden), bf16),
        d_in2=vm((steps, rows, hidden), f32),
        g=vm((rows, latent), f32),
        d_g1=vm((steps, rows, latent), f32),
        d_g2=vm((steps, rows, latent), f32),
        low2=vm((rows, latent), bf16),
        cd=vm((rows, latent), bf16),
        to_g=vm((rows, latent), f32),
        d_out=vm((rows, latent), bf16),
    )


def local_kernel(work_names, *refs):
    ins = dict(zip(names, refs))
    err_ref, up_ref, down_ref = refs[len(names) : len(names) + 3]
    work = dict(zip(work_names, refs[len(names) + 3 :]))
    steps = ins["mults"].shape[0]
    prepare(ins, work)

    @pl.loop(0, steps)
    def _(n):
        forward(n, ins, work)

    err_ref[...] = work["err"][...]

    @pl.loop(0, steps - 1)
    def _(i):
        n = steps - 1 - i
        back_drift(n, ins, work)
        back_pre(n, ins, work)
        back_state(n, ins, work)

    back_drift(0, ins, work)
    back_pre(0, ins, work)
    for j in blocks(down_ref.shape[1]):
        down_ref[:, j] = dot(work["cd_t"][...], work["hid"][:, j])
        up_ref[:, j] = dot(work["low_t"][...], work["cpre"][:, j])


def whole_kernel(work_names, groups, members, total_count, *refs):
    ins = dict(zip(names, refs))
    err_ref, up_ref, down_ref = refs[len(names) : len(names) + 3]
    work = dict(zip(work_names, refs[len(names) + 3 :]))
    steps = ins["mults"].shape[0]
    latent, hidden = ins["w_up"].shape
    outer = members // (inner * cores)
    chunk = latent // members
    half = chunk // groups
    x = lax.axis_index("grp")
    place = lax.axis_index("dp")
    core = lax.rem(place, cores)
    y = lax.rem(place // cores, inner)
    z = place // (cores * inner)

    def at(g, o, i, c):
        return (g, (o * inner + i) * cores + c)

    mate = at(x, z, y, 1 - core)
    beside = at(x, z, 1 - y, core)
    across = at(1 - x, z, y, core)
    along = [at(x, lax.rem(z + 1 + k, outer), y, core) for k in range(outer - 1)]
    partners = [mate, beside, across] + along

    barrier = pltpu.get_barrier_semaphore()
    for partner in partners:
        pl.semaphore_signal(barrier, inc=1, device_id=partner, device_id_type=MESH)

    pending = {}

    def send(key, source, target, device):
        number = len(pending)
        pending[key] = pltpu.make_async_remote_copy(
            src_ref=source,
            dst_ref=target,
            send_sem=work["sent"].at[number],
            recv_sem=work["got"].at[number],
            device_id=device,
            device_id_type=MESH,
        )
        pending[key].start()

    prepare(ins, work)

    @pl.loop(0, steps)
    def _(n):
        forward(n, ins, work)

    pl.semaphore_wait(barrier, len(partners))
    err_in = work["err_in"]
    err_sum = work["err_sum"]
    send("e0", work["err"], err_in.at[0], mate)

    @pl.loop(0, steps - 1)
    def _(i):
        n = steps - 1 - i
        back_drift(n, ins, work)
        back_pre(n, ins, work)
        back_state(n, ins, work)

    pending["e0"].wait_recv()
    err_sum[0] = work["err"][...] + err_in[0]
    send("e1", err_sum.at[0], err_in.at[1], beside)
    back_drift(0, ins, work)

    grads = work["grads"]
    in0, in1, in2, in3, in4 = (work[f"arrive{i}"] for i in range(5))
    mine = pl.ds(pl.multiple_of(x * half, half), half)
    other = pl.ds(pl.multiple_of((1 - x) * half, half), half)
    span = latent // outer

    def product(a, k):
        left, right = (("cd_t", "hid"), ("low_t", "cpre"))[a]
        piece = lax.rem(z + 1 + k, outer)
        rows = pl.ds(pl.multiple_of(piece * span, span), span)
        for j in blocks(hidden):
            value = dot(work[left][rows, :], work[right][:, j])
            grads[a, k, :, :, :, j] = value.reshape(inner, cores, chunk, value.shape[1])
        send((0, a, k), grads.at[a, k, :, 1 - core], in0.at[a, k], mate)

    def first(a, k):
        pending[0, a, k].wait_recv()
        grads[a, k, :, core] = grads[a, k, :, core] + in0[a, k]
        if a == 0:
            send((1, a, k), grads.at[a, k, 1 - y, core], in1.at[k], beside)
        else:
            send((1, a, k), grads.at[a, k, :, core, other], work["arrive1b"].at[k], across)

    def second(a, k):
        pending[1, a, k].wait_recv()
        if a == 0:
            grads[a, k, y, core] = grads[a, k, y, core] + in1[k]
            send((2, a, k), grads.at[a, k, y, core, other], in2.at[a, k], across)
        else:
            grads[a, k, :, core, mine] = grads[a, k, :, core, mine] + work["arrive1b"][k]
            send((2, a, k), grads.at[a, k, 1 - y, core, mine], in2.at[a, k], beside)

    def third(a, k):
        pending[2, a, k].wait_recv()
        grads[a, k, y, core, mine] = grads[a, k, y, core, mine] + in2[a, k]
        if k < outer - 1:
            send((3, a, k), grads.at[a, k, y, core, mine], in3.at[a, k], along[k])

    def fourth(a):
        value = grads[a, outer - 1, y, core, mine]
        for k in range(outer - 1):
            pending[3, a, k].wait_recv()
            value = value + in3[a, k]
        work["done"][a] = value
        send((4, a), work["done"].at[a], in4.at[a], across)
        (down_ref, up_ref)[a][mine, :] = value

    def fifth(a):
        pending[4, a].wait_recv()
        (down_ref, up_ref)[a][other, :] = in4[a]

    for k in range(outer):
        product(0, k)
    first(0, 0)
    back_pre(0, ins, work)
    for k in range(1, outer):
        first(0, k)
    for k in range(outer):
        product(1, k)
        if k > 0:
            first(1, k - 1)
    first(1, outer - 1)
    pending["e1"].wait_recv()
    err_sum[1] = err_sum[0] + err_in[1]
    send("e2", err_sum.at[1], err_in.at[2], across)
    for k in range(outer):
        second(0, k)
        second(1, k)
        if k == 1:
            pending["e2"].wait_recv()
            err_sum[2] = err_sum[1] + err_in[2]
            for i in range(outer - 1):
                send(("e3", i), err_sum.at[2], err_in.at[3 + i], along[i])
        if k > 0:
            third(0, k - 1)
            third(1, k - 1)
    third(0, outer - 1)
    third(1, outer - 1)
    fourth(0)
    fourth(1)
    total = err_sum[2]
    for i in range(outer - 1):
        pending["e3", i].wait_recv()
        total = total + err_in[3 + i]
    norms = jnp.sqrt(jnp.sum(total, axis=1, keepdims=True) * (1.0 / total_count))
    for n in range(steps):
        err_ref[n] = jnp.sum(norms[n : n + 1, 0:1])
    fifth(0)
    fifth(1)
    for copy in pending.values():
        copy.wait_send()


def per_device(
    start_state, w_up, b_up, w_down, w_spread, w_scale, b_scale, brownian_noise, step_mults,
    accept_flags, cotangent,
):
    groups = lax.axis_size("grp")
    members = lax.axis_size("dp")
    rows, latent = start_state.shape
    hidden = w_up.shape[1]
    steps = brownian_noise.shape[0]
    total_count = rows * latent * groups * members
    args = (
        start_state, w_up, b_up[None, :], w_down, w_spread, w_scale, b_scale[None, :],
        brownian_noise, step_mults, accept_flags, cotangent,
    )
    work = work_shapes(steps, rows, latent, hidden)
    vmem = pl.BlockSpec(memory_space=pltpu.VMEM)
    chunk = latent // members
    paired = groups == 2 and members % (inner * cores) == 0 and members > inner * cores
    if not paired or chunk % (8 * groups) != 0:
        err, up, down = pl.pallas_call(
            functools.partial(local_kernel, tuple(work)),
            out_shape=(
                jax.ShapeDtypeStruct((8, 128), f32),
                jax.ShapeDtypeStruct((latent, hidden), f32),
                jax.ShapeDtypeStruct((latent, hidden), f32),
            ),
            in_specs=[vmem] * len(args),
            out_specs=(vmem,) * 3,
            scratch_shapes=list(work.values()),
            compiler_params=pltpu.CompilerParams(vmem_limit_bytes=56 * 2**20),
        )(*args)
        totals = lax.psum(jnp.sum(err[:steps], axis=1), ("grp", "dp"))
        up, down = (
            lax.psum_scatter(g, "dp", scatter_dimension=0, tiled=True) for g in (up, down)
        )
        up, down = lax.psum((up, down), "grp")
        return (jnp.sqrt(totals / total_count), up, down)
    outer = members // (inner * cores)
    half = chunk // groups
    vm = pltpu.VMEM
    copies = 6 * outer + 2 * (outer - 1) + 2 + 3 + outer - 1
    work.update(
        grads=vm((2, outer, inner, cores, chunk, hidden), f32),
        arrive0=vm((2, outer, inner, chunk, hidden), f32),
        arrive1=vm((outer, chunk, hidden), f32),
        arrive1b=vm((outer, inner, half, hidden), f32),
        arrive2=vm((2, outer, half, hidden), f32),
        arrive3=vm((2, outer - 1, half, hidden), f32),
        arrive4=vm((2, half, hidden), f32),
        done=vm((2, half, hidden), f32),
        err_in=vm((2 + outer, 8, 128), f32),
        err_sum=vm((3, 8, 128), f32),
        sent=pltpu.SemaphoreType.DMA((copies,)),
        got=pltpu.SemaphoreType.DMA((copies,)),
    )
    return pl.pallas_call(
        functools.partial(whole_kernel, tuple(work), groups, members, total_count),
        out_shape=(
            jax.ShapeDtypeStruct((steps,), f32),
            jax.ShapeDtypeStruct((chunk, hidden), f32),
            jax.ShapeDtypeStruct((chunk, hidden), f32),
        ),
        in_specs=[vmem] * len(args),
        out_specs=(pl.BlockSpec(memory_space=pltpu.SMEM), vmem, vmem),
        scratch_shapes=list(work.values()),
        compiler_params=pltpu.CompilerParams(
            vmem_limit_bytes=56 * 2**20, collective_id=0, has_side_effects=True
        ),
    )(*args)


def solution(mesh):
    in_specs = (
        P(("grp", "dp"), None),
        P(),
        P(),
        P(),
        P(),
        P(),
        P(),
        P(None, ("grp", "dp"), None),
        P(None, ("grp", "dp")),
        P(None, ("grp", "dp")),
        P(("grp", "dp"), None),
    )
    out_specs = (P(), P("dp", None), P("dp", None))
    return jax.shard_map(
        per_device, mesh=mesh, in_specs=in_specs, out_specs=out_specs, check_vma=False
    )
```

```python
import functools

import jax
import jax.numpy as jnp
from jax import lax
from jax.experimental import pallas as pl
from jax.experimental.pallas import tpu as pltpu
from jax.sharding import PartitionSpec as P

base_step = 0.05
abs_tol = 0.01
rel_tol = 0.01
cores = 2
inner = 2
MESH = pl.DeviceIdType.MESH
f32 = jnp.float32
bf16 = jnp.bfloat16


def sigmoid(x):
    return 0.5 * jnp.tanh(0.5 * x) + 0.5


def dot(a, b):
    return jnp.dot(a, b, preferred_element_type=f32)


def dot_t(a, b):
    return lax.dot_general(a, b, (((1,), (1,)), ((), ())), preferred_element_type=f32)


def blocks(extent, width=256):
    width = min(width, extent)
    return [slice(at, at + width) for at in range(0, extent, width)]


def silu_pair(x):
    s = sigmoid(x)
    y = x * s
    return y.astype(bf16), s + y * (1.0 - s)


def prepare(ins, work):
    steps, rows = ins["mults"].shape
    table = work["table"]
    table[...] = jnp.zeros_like(table)
    table[0:steps, :] = ins["mults"][...].astype(f32) * base_step
    table[steps : 2 * steps, :] = ins["flags"][...].astype(f32)
    turned = table[...].T
    lanes = table.shape[0]
    for n in range(steps):
        h = jnp.broadcast_to(turned[:, n : n + 1], (rows, lanes))
        work["h"][n] = h
        work["r"][n] = jnp.sqrt(h)
        work["keep"][n] = jnp.broadcast_to(turned[:, steps + n : steps + n + 1], (rows, lanes))
    work["cur"][...] = ins["start"][...].astype(f32)
    work["cot"][...] = ins["cot"][...].astype(f32)
    work["err"][...] = jnp.zeros_like(work["err"])


def forward(n, ins, work):
    rows, latent = work["cur"].shape
    hidden = ins["w_up"].shape[1]
    at = pl.ds(pl.multiple_of(n * rows, rows), rows)
    h = work["h"][n][:, 0:1]
    r = work["r"][n][:, 0:1]
    keep = work["keep"][n][:, 0:1]
    cur = work["cur"][...]
    low = cur.astype(bf16)
    work["low_t"][:, at] = cur.T.astype(bf16)
    for j in blocks(hidden):
        work["in1"][:, j], work["d_in1"][n, :, j] = silu_pair(dot(low, ins["w_spread"][:, j]))
    for j in blocks(hidden):
        x = dot(low, ins["w_up"][:, j]) + ins["b_up"][:, j]
        work["hid"][at, j], work["d_hid"][n, :, j] = silu_pair(x)
    for j in blocks(latent):
        s = sigmoid(dot(work["in1"][...], ins["w_scale"][:, j]) + ins["b_scale"][:, j])
        g = 0.6 * s
        work["g"][:, j] = g
        work["d_g1"][n, :, j] = g * (1.0 - s)
        work["low2"][:, j] = (work["cur"][:, j] + g * r).astype(bf16)
    for j in blocks(hidden):
        work["in2"][:, j], work["d_in2"][n, :, j] = silu_pair(
            dot(work["low2"][...], ins["w_spread"][:, j])
        )
    total = jnp.zeros((1, 128), f32)
    for j in blocks(latent):
        s = sigmoid(dot(work["in2"][...], ins["w_scale"][:, j]) + ins["b_scale"][:, j])
        gbar = 0.6 * s
        work["d_g2"][n, :, j] = gbar * (1.0 - s)
        drift = dot(work["hid"][at, :], ins["w_down"][:, j])
        noise = ins["noise"][n, :, j].astype(f32)
        g = work["g"][:, j]
        c = work["cur"][:, j]
        milstein = (gbar - g) * (0.5 * r * (noise * noise - 1.0))
        scaled = milstein / (abs_tol + rel_tol * jnp.abs(c))
        part = jnp.sum(scaled * scaled, axis=0, keepdims=True)
        for i in blocks(part.shape[1], 128):
            total = total + part[:, i]
        proposal = c + drift * h + g * (r * noise) + milstein
        work["cur"][:, j] = jnp.where(keep > 0.5, proposal, c)
    work["err"][pl.ds(n, 1), :] = total


def back_drift(n, ins, work):
    rows, latent = work["cur"].shape
    at = pl.ds(pl.multiple_of(n * rows, rows), rows)
    cd = work["cot"][...] * (work["keep"][n][:, 0:1] * work["h"][n][:, 0:1])
    work["cd"][...] = cd.astype(bf16)
    work["cd_t"][:, at] = cd.T.astype(bf16)


def back_pre(n, ins, work):
    rows, latent = work["cur"].shape
    hidden = ins["w_up"].shape[1]
    at = pl.ds(pl.multiple_of(n * rows, rows), rows)
    for j in blocks(hidden):
        back = dot_t(work["cd"][...], ins["w_down"][j, :])
        work["cpre"][at, j] = (back * work["d_hid"][n, :, j]).astype(bf16)


def back_state(n, ins, work):
    rows, latent = work["cur"].shape
    hidden = ins["w_up"].shape[1]
    at = pl.ds(pl.multiple_of(n * rows, rows), rows)
    r = work["r"][n][:, 0:1]
    keep = work["keep"][n][:, 0:1]
    for j in blocks(latent):
        noise = ins["noise"][n, :, j].astype(f32)
        ck = keep * work["cot"][:, j]
        to_bar = ck * (0.5 * r * (noise * noise - 1.0))
        work["to_g"][:, j] = ck * (r * noise) - to_bar
        work["d_out"][:, j] = (to_bar * work["d_g2"][n, :, j]).astype(bf16)
    for j in blocks(hidden):
        back = dot_t(work["d_out"][...], ins["w_scale"][j, :]).astype(bf16).astype(f32)
        work["in2"][:, j] = (back * work["d_in2"][n, :, j]).astype(bf16)
    for j in blocks(latent):
        back = dot_t(work["in2"][...], ins["w_spread"][j, :]).astype(bf16).astype(f32)
        work["g"][:, j] = back
        work["d_out"][:, j] = (
            (work["to_g"][:, j] + back * r) * work["d_g1"][n, :, j]
        ).astype(bf16)
    for j in blocks(hidden):
        back = dot_t(work["d_out"][...], ins["w_scale"][j, :]).astype(bf16).astype(f32)
        work["in1"][:, j] = (back * work["d_in1"][n, :, j]).astype(bf16)
    for j in blocks(latent):
        back = dot_t(work["in1"][...], ins["w_spread"][j, :]).astype(bf16).astype(f32)
        through = dot_t(work["cpre"][at, :], ins["w_up"][j, :])
        work["cot"][:, j] = work["cot"][:, j] + work["g"][:, j] + back + through


names = (
    "start", "w_up", "b_up", "w_down", "w_spread", "w_scale", "b_scale", "noise", "mults",
    "flags", "cot",
)


def work_shapes(steps, rows, latent, hidden):
    vm = pltpu.VMEM
    return dict(
        table=vm((128, rows), f32),
        h=vm((steps, rows, 128), f32),
        r=vm((steps, rows, 128), f32),
        keep=vm((steps, rows, 128), f32),
        cur=vm((rows, latent), f32),
        cot=vm((rows, latent), f32),
        err=vm((8, 128), f32),
        low_t=vm((latent, steps * rows), bf16),
        cd_t=vm((latent, steps * rows), bf16),
        hid=vm((steps * rows, hidden), bf16),
        cpre=vm((steps * rows, hidden), bf16),
        d_hid=vm((steps, rows, hidden), f32),
        in1=vm((rows, hidden), bf16),
        d_in1=vm((steps, rows, hidden), f32),
        in2=vm((rows, hidden), bf16),
        d_in2=vm((steps, rows, hidden), f32),
        g=vm((rows, latent), f32),
        d_g1=vm((steps, rows, latent), f32),
        d_g2=vm((steps, rows, latent), f32),
        low2=vm((rows, latent), bf16),
        cd=vm((rows, latent), bf16),
        to_g=vm((rows, latent), f32),
        d_out=vm((rows, latent), bf16),
    )


def local_kernel(work_names, *refs):
    ins = dict(zip(names, refs))
    err_ref, up_ref, down_ref = refs[len(names) : len(names) + 3]
    work = dict(zip(work_names, refs[len(names) + 3 :]))
    steps = ins["mults"].shape[0]
    prepare(ins, work)

    @pl.loop(0, steps)
    def _(n):
        forward(n, ins, work)

    err_ref[...] = work["err"][...]

    @pl.loop(0, steps - 1)
    def _(i):
        n = steps - 1 - i
        back_drift(n, ins, work)
        back_pre(n, ins, work)
        back_state(n, ins, work)

    back_drift(0, ins, work)
    back_pre(0, ins, work)
    for j in blocks(down_ref.shape[1]):
        down_ref[:, j] = dot(work["cd_t"][...], work["hid"][:, j])
        up_ref[:, j] = dot(work["low_t"][...], work["cpre"][:, j])


def whole_kernel(work_names, groups, members, total_count, *refs):
    ins = dict(zip(names, refs))
    err_ref, up_ref, down_ref = refs[len(names) : len(names) + 3]
    work = dict(zip(work_names, refs[len(names) + 3 :]))
    steps = ins["mults"].shape[0]
    latent, hidden = ins["w_up"].shape
    outer = members // (inner * cores)
    chunk = latent // members
    half = chunk // groups
    x = lax.axis_index("grp")
    place = lax.axis_index("dp")
    core = lax.rem(place, cores)
    y = lax.rem(place // cores, inner)
    z = place // (cores * inner)

    def at(g, o, i, c):
        return (g, (o * inner + i) * cores + c)

    mate = at(x, z, y, 1 - core)
    beside = at(x, z, 1 - y, core)
    across = at(1 - x, z, y, core)
    along = [at(x, lax.rem(z + 1 + k, outer), y, core) for k in range(outer - 1)]
    partners = [mate, beside, across] + along

    barrier = pltpu.get_barrier_semaphore()
    for partner in partners:
        pl.semaphore_signal(barrier, inc=1, device_id=partner, device_id_type=MESH)

    pending = {}

    def send(key, source, target, device):
        number = len(pending)
        pending[key] = pltpu.make_async_remote_copy(
            src_ref=source,
            dst_ref=target,
            send_sem=work["sent"].at[number],
            recv_sem=work["got"].at[number],
            device_id=device,
            device_id_type=MESH,
        )
        pending[key].start()

    prepare(ins, work)

    @pl.loop(0, steps)
    def _(n):
        forward(n, ins, work)

    pl.semaphore_wait(barrier, len(partners))
    err_in = work["err_in"]
    err_sum = work["err_sum"]
    send("e0", work["err"], err_in.at[0], mate)

    @pl.loop(0, steps - 1)
    def _(i):
        n = steps - 1 - i
        back_drift(n, ins, work)
        back_pre(n, ins, work)
        back_state(n, ins, work)

    pending["e0"].wait_recv()
    err_sum[0] = work["err"][...] + err_in[0]
    send("e1", err_sum.at[0], err_in.at[1], beside)
    back_drift(0, ins, work)

    grads = work["grads"]
    in0, in1, in2, in3, in4 = (work[f"arrive{i}"] for i in range(5))
    in1b = work["arrive1b"]
    mine = pl.ds(pl.multiple_of(x * half, half), half)
    other = pl.ds(pl.multiple_of((1 - x) * half, half), half)
    span = latent // outer

    def product(a, k):
        left, right = (("cd_t", "hid"), ("low_t", "cpre"))[a]
        piece = lax.rem(z + 1 + k, outer)
        rows = pl.ds(pl.multiple_of(piece * span, span), span)
        for j in blocks(hidden):
            value = dot(work[left][rows, :], work[right][:, j])
            grads[a, k, :, :, :, j] = value.reshape(inner, cores, chunk, value.shape[1])
        send((0, a, k), grads.at[a, k, :, 1 - core], in0.at[a, k], mate)

    def y_first(a, k):
        return (a == 0) if k == outer - 1 else (a + k) % 2 == 0

    def first(a, k):
        pending[0, a, k].wait_recv()
        grads[a, k, :, core] = grads[a, k, :, core] + in0[a, k]
        if y_first(a, k):
            send((1, a, k), grads.at[a, k, 1 - y, core], in1.at[a, k], beside)
        else:
            send((1, a, k), grads.at[a, k, :, core, other], in1b.at[a, k], across)

    def second(a, k):
        pending[1, a, k].wait_recv()
        if y_first(a, k):
            grads[a, k, y, core] = grads[a, k, y, core] + in1[a, k]
            send((2, a, k), grads.at[a, k, y, core, other], in2.at[a, k], across)
        else:
            grads[a, k, :, core, mine] = grads[a, k, :, core, mine] + in1b[a, k]
            send((2, a, k), grads.at[a, k, 1 - y, core, mine], in2.at[a, k], beside)

    def third(a, k):
        pending[2, a, k].wait_recv()
        grads[a, k, y, core, mine] = grads[a, k, y, core, mine] + in2[a, k]
        if k < outer - 1:
            send((3, a, k), grads.at[a, k, y, core, mine], in3.at[a, k], along[k])

    def fourth(a):
        value = grads[a, outer - 1, y, core, mine]
        for k in range(outer - 1):
            pending[3, a, k].wait_recv()
            value = value + in3[a, k]
        work["done"][a] = value
        send((4, a), work["done"].at[a], in4.at[a], across)
        (down_ref, up_ref)[a][mine, :] = value

    def fifth(a):
        pending[4, a].wait_recv()
        (down_ref, up_ref)[a][other, :] = in4[a]

    order = [(0, k) for k in range(outer - 1)] + [(1, k) for k in range(outer - 1)]
    order += [(0, outer - 1), (1, outer - 1)]
    for k in range(outer):
        product(0, k)
    first(*order[0])
    first(*order[1])
    back_pre(0, ins, work)
    for k in range(outer):
        product(1, k)
    pending["e1"].wait_recv()
    err_sum[1] = err_sum[0] + err_in[1]
    send("e2", err_sum.at[1], err_in.at[2], across)
    count = len(order)
    for at_pair in range(2, count + 4, 2):
        for i in (at_pair, at_pair + 1):
            if i < count:
                first(*order[i])
        for i in (at_pair - 2, at_pair - 1):
            if i < count:
                second(*order[i])
        for i in (at_pair - 4, at_pair - 3):
            if 0 <= i < count:
                third(*order[i])
        if at_pair == 4:
            pending["e2"].wait_recv()
            err_sum[2] = err_sum[1] + err_in[2]
            for i in range(outer - 1):
                send(("e3", i), err_sum.at[2], err_in.at[3 + i], along[i])
    fourth(0)
    fourth(1)
    total = err_sum[2]
    for i in range(outer - 1):
        pending["e3", i].wait_recv()
        total = total + err_in[3 + i]
    norms = jnp.sqrt(jnp.sum(total, axis=1, keepdims=True) * (1.0 / total_count))
    for n in range(steps):
        err_ref[n] = jnp.sum(norms[n : n + 1, 0:1])
    fifth(0)
    fifth(1)
    for copy in pending.values():
        copy.wait_send()


def hand_over(err_ref, up_ref, down_ref, err_out, up_out, down_out, sems):
    copies = [
        pltpu.make_async_copy(up_ref, up_out, sems.at[0]),
        pltpu.make_async_copy(down_ref, down_out, sems.at[1]),
    ]
    for copy in copies:
        copy.start()
    for n in range(err_out.shape[0]):
        err_out[n] = err_ref[n]
    for copy in copies:
        copy.wait()


def per_device(
    start_state, w_up, b_up, w_down, w_spread, w_scale, b_scale, brownian_noise, step_mults,
    accept_flags, cotangent,
):
    groups = lax.axis_size("grp")
    members = lax.axis_size("dp")
    rows, latent = start_state.shape
    hidden = w_up.shape[1]
    steps = brownian_noise.shape[0]
    total_count = rows * latent * groups * members
    args = (
        start_state, w_up, b_up[None, :], w_down, w_spread, w_scale, b_scale[None, :],
        brownian_noise, step_mults, accept_flags, cotangent,
    )
    work = work_shapes(steps, rows, latent, hidden)
    vmem = pl.BlockSpec(memory_space=pltpu.VMEM)
    chunk = latent // members
    paired = groups == 2 and members % (inner * cores) == 0 and members > inner * cores
    if not paired or chunk % (8 * groups) != 0:
        err, up, down = pl.pallas_call(
            functools.partial(local_kernel, tuple(work)),
            out_shape=(
                jax.ShapeDtypeStruct((8, 128), f32),
                jax.ShapeDtypeStruct((latent, hidden), f32),
                jax.ShapeDtypeStruct((latent, hidden), f32),
            ),
            in_specs=[vmem] * len(args),
            out_specs=(vmem,) * 3,
            scratch_shapes=list(work.values()),
            compiler_params=pltpu.CompilerParams(vmem_limit_bytes=56 * 2**20),
        )(*args)
        totals = lax.psum(jnp.sum(err[:steps], axis=1), ("grp", "dp"))
        up, down = (
            lax.psum_scatter(g, "dp", scatter_dimension=0, tiled=True) for g in (up, down)
        )
        up, down = lax.psum((up, down), "grp")
        return (jnp.sqrt(totals / total_count), up, down)
    outer = members // (inner * cores)
    half = chunk // groups
    vm = pltpu.VMEM
    copies = 6 * outer + 2 * (outer - 1) + 2 + 3 + outer - 1
    work.update(
        grads=vm((2, outer, inner, cores, chunk, hidden), f32),
        arrive0=vm((2, outer, inner, chunk, hidden), f32),
        arrive1=vm((2, outer, chunk, hidden), f32),
        arrive1b=vm((2, outer, inner, half, hidden), f32),
        arrive2=vm((2, outer, half, hidden), f32),
        arrive3=vm((2, outer - 1, half, hidden), f32),
        arrive4=vm((2, half, hidden), f32),
        done=vm((2, half, hidden), f32),
        err_in=vm((2 + outer, 8, 128), f32),
        err_sum=vm((3, 8, 128), f32),
        sent=pltpu.SemaphoreType.DMA((copies,)),
        got=pltpu.SemaphoreType.DMA((copies,)),
    )
    out_shape = (
        jax.ShapeDtypeStruct((steps,), f32),
        jax.ShapeDtypeStruct((chunk, hidden), f32),
        jax.ShapeDtypeStruct((chunk, hidden), f32),
    )
    results = pl.pallas_call(
        functools.partial(whole_kernel, tuple(work), groups, members, total_count),
        out_shape=out_shape,
        in_specs=[vmem] * len(args),
        out_specs=(pl.BlockSpec(memory_space=pltpu.SMEM), vmem, vmem),
        scratch_shapes=list(work.values()),
        compiler_params=pltpu.CompilerParams(
            vmem_limit_bytes=56 * 2**20, collective_id=0, has_side_effects=True
        ),
    )(*args)
    smem = pl.BlockSpec(memory_space=pltpu.SMEM)
    anywhere = pl.BlockSpec(memory_space=pl.ANY)
    return pl.pallas_call(
        hand_over,
        out_shape=out_shape,
        in_specs=[smem, anywhere, anywhere],
        out_specs=(smem, anywhere, anywhere),
        scratch_shapes=[pltpu.SemaphoreType.DMA((2,))],
        compiler_params=pltpu.CompilerParams(vmem_limit_bytes=60 * 2**20),
    )(*results)


def solution(mesh):
    in_specs = (
        P(("grp", "dp"), None),
        P(),
        P(),
        P(),
        P(),
        P(),
        P(),
        P(None, ("grp", "dp"), None),
        P(None, ("grp", "dp")),
        P(None, ("grp", "dp")),
        P(("grp", "dp"), None),
    )
    out_specs = (P(), P("dp", None), P("dp", None))
    return jax.shard_map(
        per_device, mesh=mesh, in_specs=in_specs, out_specs=out_specs, check_vma=False
    )
```

```python
import functools

import jax
import jax.numpy as jnp
from jax import lax
from jax.experimental import pallas as pl
from jax.experimental.pallas import tpu as pltpu
from jax.sharding import PartitionSpec as P

base_step = 0.05
abs_tol = 0.01
rel_tol = 0.01
cores = 2
inner = 2
MESH = pl.DeviceIdType.MESH
f32 = jnp.float32
bf16 = jnp.bfloat16


def sigmoid(x):
    return 0.5 * jnp.tanh(0.5 * x) + 0.5


def dot(a, b):
    return jnp.dot(a, b, preferred_element_type=f32)


def dot_t(a, b):
    return lax.dot_general(a, b, (((1,), (1,)), ((), ())), preferred_element_type=f32)


def blocks(extent, width=256):
    width = min(width, extent)
    return [slice(at, at + width) for at in range(0, extent, width)]


def silu_pair(x):
    s = sigmoid(x)
    y = x * s
    return y.astype(bf16), s + y * (1.0 - s)


def prepare(ins, work):
    steps, rows = ins["mults"].shape
    table = work["table"]
    table[...] = jnp.zeros_like(table)
    table[0:steps, :] = ins["mults"][...].astype(f32) * base_step
    table[steps : 2 * steps, :] = ins["flags"][...].astype(f32)
    turned = table[...].T
    lanes = table.shape[0]
    for n in range(steps):
        h = jnp.broadcast_to(turned[:, n : n + 1], (rows, lanes))
        work["h"][n] = h
        work["r"][n] = jnp.sqrt(h)
        work["keep"][n] = jnp.broadcast_to(turned[:, steps + n : steps + n + 1], (rows, lanes))
    work["cur"][...] = ins["start"][...].astype(f32)
    work["cot"][...] = ins["cot"][...].astype(f32)
    work["err"][...] = jnp.zeros_like(work["err"])


def forward(n, ins, work):
    rows, latent = work["cur"].shape
    hidden = ins["w_up"].shape[1]
    at = pl.ds(pl.multiple_of(n * rows, rows), rows)
    h = work["h"][n][:, 0:1]
    r = work["r"][n][:, 0:1]
    keep = work["keep"][n][:, 0:1]
    cur = work["cur"][...]
    low = cur.astype(bf16)
    work["low_t"][:, at] = cur.T.astype(bf16)
    for j in blocks(hidden):
        work["in1"][:, j], work["d_in1"][n, :, j] = silu_pair(dot(low, ins["w_spread"][:, j]))
    for j in blocks(hidden):
        x = dot(low, ins["w_up"][:, j]) + ins["b_up"][:, j]
        work["hid"][at, j], work["d_hid"][n, :, j] = silu_pair(x)
    for j in blocks(latent):
        s = sigmoid(dot(work["in1"][...], ins["w_scale"][:, j]) + ins["b_scale"][:, j])
        g = 0.6 * s
        work["g"][:, j] = g
        work["d_g1"][n, :, j] = g * (1.0 - s)
        work["low2"][:, j] = (work["cur"][:, j] + g * r).astype(bf16)
    for j in blocks(hidden):
        work["in2"][:, j], work["d_in2"][n, :, j] = silu_pair(
            dot(work["low2"][...], ins["w_spread"][:, j])
        )
    total = jnp.zeros((1, 128), f32)
    for j in blocks(latent):
        s = sigmoid(dot(work["in2"][...], ins["w_scale"][:, j]) + ins["b_scale"][:, j])
        gbar = 0.6 * s
        work["d_g2"][n, :, j] = gbar * (1.0 - s)
        drift = dot(work["hid"][at, :], ins["w_down"][:, j])
        noise = ins["noise"][n, :, j].astype(f32)
        g = work["g"][:, j]
        c = work["cur"][:, j]
        milstein = (gbar - g) * (0.5 * r * (noise * noise - 1.0))
        scaled = milstein / (abs_tol + rel_tol * jnp.abs(c))
        part = jnp.sum(scaled * scaled, axis=0, keepdims=True)
        for i in blocks(part.shape[1], 128):
            total = total + part[:, i]
        proposal = c + drift * h + g * (r * noise) + milstein
        work["cur"][:, j] = jnp.where(keep > 0.5, proposal, c)
    work["err"][pl.ds(n, 1), :] = total


def back_drift(n, ins, work):
    rows, latent = work["cur"].shape
    at = pl.ds(pl.multiple_of(n * rows, rows), rows)
    cd = work["cot"][...] * (work["keep"][n][:, 0:1] * work["h"][n][:, 0:1])
    work["cd"][...] = cd.astype(bf16)
    work["cd_t"][:, at] = cd.T.astype(bf16)


def back_pre(n, ins, work):
    rows, latent = work["cur"].shape
    hidden = ins["w_up"].shape[1]
    at = pl.ds(pl.multiple_of(n * rows, rows), rows)
    for j in blocks(hidden):
        back = dot_t(work["cd"][...], ins["w_down"][j, :])
        work["cpre"][at, j] = (back * work["d_hid"][n, :, j]).astype(bf16)


def back_state(n, ins, work):
    rows, latent = work["cur"].shape
    hidden = ins["w_up"].shape[1]
    at = pl.ds(pl.multiple_of(n * rows, rows), rows)
    r = work["r"][n][:, 0:1]
    keep = work["keep"][n][:, 0:1]
    for j in blocks(latent):
        noise = ins["noise"][n, :, j].astype(f32)
        ck = keep * work["cot"][:, j]
        to_bar = ck * (0.5 * r * (noise * noise - 1.0))
        work["to_g"][:, j] = ck * (r * noise) - to_bar
        work["d_out"][:, j] = (to_bar * work["d_g2"][n, :, j]).astype(bf16)
    for j in blocks(hidden):
        back = dot_t(work["d_out"][...], ins["w_scale"][j, :]).astype(bf16).astype(f32)
        work["in2"][:, j] = (back * work["d_in2"][n, :, j]).astype(bf16)
    for j in blocks(latent):
        back = dot_t(work["in2"][...], ins["w_spread"][j, :]).astype(bf16).astype(f32)
        work["g"][:, j] = back
        work["d_out"][:, j] = (
            (work["to_g"][:, j] + back * r) * work["d_g1"][n, :, j]
        ).astype(bf16)
    for j in blocks(hidden):
        back = dot_t(work["d_out"][...], ins["w_scale"][j, :]).astype(bf16).astype(f32)
        work["in1"][:, j] = (back * work["d_in1"][n, :, j]).astype(bf16)
    for j in blocks(latent):
        back = dot_t(work["in1"][...], ins["w_spread"][j, :]).astype(bf16).astype(f32)
        through = dot_t(work["cpre"][at, :], ins["w_up"][j, :])
        work["cot"][:, j] = work["cot"][:, j] + work["g"][:, j] + back + through


names = (
    "start", "w_up", "b_up", "w_down", "w_spread", "w_scale", "b_scale", "noise", "mults",
    "flags", "cot",
)


def work_shapes(steps, rows, latent, hidden):
    vm = pltpu.VMEM
    return dict(
        table=vm((128, rows), f32),
        h=vm((steps, rows, 128), f32),
        r=vm((steps, rows, 128), f32),
        keep=vm((steps, rows, 128), f32),
        cur=vm((rows, latent), f32),
        cot=vm((rows, latent), f32),
        err=vm((8, 128), f32),
        low_t=vm((latent, steps * rows), bf16),
        cd_t=vm((latent, steps * rows), bf16),
        hid=vm((steps * rows, hidden), bf16),
        cpre=vm((steps * rows, hidden), bf16),
        d_hid=vm((steps, rows, hidden), f32),
        in1=vm((rows, hidden), bf16),
        d_in1=vm((steps, rows, hidden), f32),
        in2=vm((rows, hidden), bf16),
        d_in2=vm((steps, rows, hidden), f32),
        g=vm((rows, latent), f32),
        d_g1=vm((steps, rows, latent), f32),
        d_g2=vm((steps, rows, latent), f32),
        low2=vm((rows, latent), bf16),
        cd=vm((rows, latent), bf16),
        to_g=vm((rows, latent), f32),
        d_out=vm((rows, latent), bf16),
    )


def local_kernel(work_names, *refs):
    ins = dict(zip(names, refs))
    err_ref, up_ref, down_ref = refs[len(names) : len(names) + 3]
    work = dict(zip(work_names, refs[len(names) + 3 :]))
    steps = ins["mults"].shape[0]
    prepare(ins, work)

    @pl.loop(0, steps)
    def _(n):
        forward(n, ins, work)

    err_ref[...] = work["err"][...]

    @pl.loop(0, steps - 1)
    def _(i):
        n = steps - 1 - i
        back_drift(n, ins, work)
        back_pre(n, ins, work)
        back_state(n, ins, work)

    back_drift(0, ins, work)
    back_pre(0, ins, work)
    for j in blocks(down_ref.shape[1]):
        down_ref[:, j] = dot(work["cd_t"][...], work["hid"][:, j])
        up_ref[:, j] = dot(work["low_t"][...], work["cpre"][:, j])


def whole_kernel(work_names, groups, members, total_count, *refs):
    ins = dict(zip(names, refs))
    err_ref, up_ref, down_ref = refs[len(names) : len(names) + 3]
    work = dict(zip(work_names, refs[len(names) + 3 :]))
    steps = ins["mults"].shape[0]
    latent, hidden = ins["w_up"].shape
    outer = members // (inner * cores)
    chunk = latent // members
    half = chunk // groups
    x = lax.axis_index("grp")
    place = lax.axis_index("dp")
    core = lax.rem(place, cores)
    y = lax.rem(place // cores, inner)
    z = place // (cores * inner)

    def at(g, o, i, c):
        return (g, (o * inner + i) * cores + c)

    mate = at(x, z, y, 1 - core)
    beside = at(x, z, 1 - y, core)
    across = at(1 - x, z, y, core)
    along = [at(x, lax.rem(z + 1 + k, outer), y, core) for k in range(outer - 1)]
    partners = [mate, beside, across] + along

    barrier = pltpu.get_barrier_semaphore()
    for partner in partners:
        pl.semaphore_signal(barrier, inc=1, device_id=partner, device_id_type=MESH)

    pending = {}

    def send(key, source, target, device):
        number = len(pending)
        pending[key] = pltpu.make_async_remote_copy(
            src_ref=source,
            dst_ref=target,
            send_sem=work["sent"].at[number],
            recv_sem=work["got"].at[number],
            device_id=device,
            device_id_type=MESH,
        )
        pending[key].start()

    prepare(ins, work)

    @pl.loop(0, steps)
    def _(n):
        forward(n, ins, work)

    pl.semaphore_wait(barrier, len(partners))
    err_in = work["err_in"]
    err_sum = work["err_sum"]
    send("e0", work["err"], err_in.at[0], mate)

    @pl.loop(0, steps - 1)
    def _(i):
        n = steps - 1 - i
        back_drift(n, ins, work)
        back_pre(n, ins, work)
        back_state(n, ins, work)

    pending["e0"].wait_recv()
    err_sum[0] = work["err"][...] + err_in[0]
    send("e1", err_sum.at[0], err_in.at[1], beside)
    back_drift(0, ins, work)

    grads = work["grads"]
    in0, in1, in2, in3, in4 = (work[f"arrive{i}"] for i in range(5))
    in1b = work["arrive1b"]
    mine = pl.ds(pl.multiple_of(x * half, half), half)
    other = pl.ds(pl.multiple_of((1 - x) * half, half), half)
    span = latent // outer

    def product(a, k):
        left, right = (("cd_t", "hid"), ("low_t", "cpre"))[a]
        piece = lax.rem(z + 1 + k, outer)
        rows = pl.ds(pl.multiple_of(piece * span, span), span)
        for j in blocks(hidden):
            value = dot(work[left][rows, :], work[right][:, j])
            grads[a, k, :, :, :, j] = value.reshape(inner, cores, chunk, value.shape[1])
        send((0, a, k), grads.at[a, k, :, 1 - core], in0.at[a, k], mate)

    def y_first(a, k):
        return (a == 0) if k == outer - 1 else (a + k) % 2 == 0

    def first(a, k):
        pending[0, a, k].wait_recv()
        grads[a, k, :, core] = grads[a, k, :, core] + in0[a, k]
        if y_first(a, k):
            send((1, a, k), grads.at[a, k, 1 - y, core], in1.at[a, k], beside)
        else:
            send((1, a, k), grads.at[a, k, :, core, other], in1b.at[a, k], across)

    def second(a, k):
        pending[1, a, k].wait_recv()
        if y_first(a, k):
            grads[a, k, y, core] = grads[a, k, y, core] + in1[a, k]
            send((2, a, k), grads.at[a, k, y, core, other], in2.at[a, k], across)
        else:
            grads[a, k, :, core, mine] = grads[a, k, :, core, mine] + in1b[a, k]
            send((2, a, k), grads.at[a, k, 1 - y, core, mine], in2.at[a, k], beside)

    def third(a, k):
        pending[2, a, k].wait_recv()
        grads[a, k, y, core, mine] = grads[a, k, y, core, mine] + in2[a, k]
        if k < outer - 1:
            send((3, a, k), grads.at[a, k, y, core, mine], in3.at[a, k], along[k])

    def fourth(a):
        value = grads[a, outer - 1, y, core, mine]
        for k in range(outer - 1):
            pending[3, a, k].wait_recv()
            value = value + in3[a, k]
        work["done"][a] = value
        send((4, a), work["done"].at[a], in4.at[a], across)
        (down_ref, up_ref)[a][mine, :] = value

    def fifth(a):
        pending[4, a].wait_recv()
        (down_ref, up_ref)[a][other, :] = in4[a]

    order = [(0, k) for k in range(outer - 1)] + [(1, k) for k in range(outer - 1)]
    order += [(0, outer - 1), (1, outer - 1)]
    for k in range(outer):
        product(0, k)
    first(*order[0])
    first(*order[1])
    back_pre(0, ins, work)
    for k in range(outer):
        product(1, k)
    pending["e1"].wait_recv()
    err_sum[1] = err_sum[0] + err_in[1]
    send("e2", err_sum.at[1], err_in.at[2], across)
    count = len(order)
    for at_pair in range(2, count + 4, 2):
        for i in (at_pair, at_pair + 1):
            if i < count:
                first(*order[i])
        for i in (at_pair - 2, at_pair - 1):
            if i < count:
                second(*order[i])
        for i in (at_pair - 4, at_pair - 3):
            if 0 <= i < count:
                third(*order[i])
        if at_pair == 4:
            pending["e2"].wait_recv()
            err_sum[2] = err_sum[1] + err_in[2]
            for i in range(outer - 1):
                send(("e3", i), err_sum.at[2], err_in.at[3 + i], along[i])
    fourth(0)
    fourth(1)
    total = err_sum[2]
    for i in range(outer - 1):
        pending["e3", i].wait_recv()
        total = total + err_in[3 + i]
    norms = jnp.sqrt(jnp.sum(total, axis=1, keepdims=True) * (1.0 / total_count))
    for n in range(steps):
        err_ref[n] = jnp.sum(norms[n : n + 1, 0:1])
    fifth(0)
    fifth(1)
    for copy in pending.values():
        copy.wait_send()


def hand_over(err_ref, up_ref, down_ref, err_out, up_out, down_out):
    up_out[...] = up_ref[...]
    down_out[...] = down_ref[...]
    for n in range(err_out.shape[0]):
        err_out[n] = err_ref[n]


def per_device(
    start_state, w_up, b_up, w_down, w_spread, w_scale, b_scale, brownian_noise, step_mults,
    accept_flags, cotangent,
):
    groups = lax.axis_size("grp")
    members = lax.axis_size("dp")
    rows, latent = start_state.shape
    hidden = w_up.shape[1]
    steps = brownian_noise.shape[0]
    total_count = rows * latent * groups * members
    args = (
        start_state, w_up, b_up[None, :], w_down, w_spread, w_scale, b_scale[None, :],
        brownian_noise, step_mults, accept_flags, cotangent,
    )
    work = work_shapes(steps, rows, latent, hidden)
    vmem = pl.BlockSpec(memory_space=pltpu.VMEM)
    chunk = latent // members
    paired = groups == 2 and members % (inner * cores) == 0 and members > inner * cores
    if not paired or chunk % (8 * groups) != 0:
        err, up, down = pl.pallas_call(
            functools.partial(local_kernel, tuple(work)),
            out_shape=(
                jax.ShapeDtypeStruct((8, 128), f32),
                jax.ShapeDtypeStruct((latent, hidden), f32),
                jax.ShapeDtypeStruct((latent, hidden), f32),
            ),
            in_specs=[vmem] * len(args),
            out_specs=(vmem,) * 3,
            scratch_shapes=list(work.values()),
            compiler_params=pltpu.CompilerParams(vmem_limit_bytes=56 * 2**20),
        )(*args)
        totals = lax.psum(jnp.sum(err[:steps], axis=1), ("grp", "dp"))
        up, down = (
            lax.psum_scatter(g, "dp", scatter_dimension=0, tiled=True) for g in (up, down)
        )
        up, down = lax.psum((up, down), "grp")
        return (jnp.sqrt(totals / total_count), up, down)
    outer = members // (inner * cores)
    half = chunk // groups
    vm = pltpu.VMEM
    copies = 6 * outer + 2 * (outer - 1) + 2 + 3 + outer - 1
    work.update(
        grads=vm((2, outer, inner, cores, chunk, hidden), f32),
        arrive0=vm((2, outer, inner, chunk, hidden), f32),
        arrive1=vm((2, outer, chunk, hidden), f32),
        arrive1b=vm((2, outer, inner, half, hidden), f32),
        arrive2=vm((2, outer, half, hidden), f32),
        arrive3=vm((2, outer - 1, half, hidden), f32),
        arrive4=vm((2, half, hidden), f32),
        done=vm((2, half, hidden), f32),
        err_in=vm((2 + outer, 8, 128), f32),
        err_sum=vm((3, 8, 128), f32),
        sent=pltpu.SemaphoreType.DMA((copies,)),
        got=pltpu.SemaphoreType.DMA((copies,)),
    )
    out_shape = (
        jax.ShapeDtypeStruct((steps,), f32),
        jax.ShapeDtypeStruct((chunk, hidden), f32),
        jax.ShapeDtypeStruct((chunk, hidden), f32),
    )
    results = pl.pallas_call(
        functools.partial(whole_kernel, tuple(work), groups, members, total_count),
        out_shape=out_shape,
        in_specs=[vmem] * len(args),
        out_specs=(pl.BlockSpec(memory_space=pltpu.SMEM), vmem, vmem),
        scratch_shapes=list(work.values()),
        compiler_params=pltpu.CompilerParams(
            vmem_limit_bytes=56 * 2**20, collective_id=0, has_side_effects=True
        ),
    )(*args)
    smem = pl.BlockSpec(memory_space=pltpu.SMEM)
    return pl.pallas_call(
        hand_over,
        out_shape=out_shape,
        in_specs=[smem, vmem, vmem],
        out_specs=(smem, vmem, vmem),
        compiler_params=pltpu.CompilerParams(vmem_limit_bytes=60 * 2**20),
    )(*results)


def solution(mesh):
    in_specs = (
        P(("grp", "dp"), None),
        P(),
        P(),
        P(),
        P(),
        P(),
        P(),
        P(None, ("grp", "dp"), None),
        P(None, ("grp", "dp")),
        P(None, ("grp", "dp")),
        P(("grp", "dp"), None),
    )
    out_specs = (P(), P("dp", None), P("dp", None))
    return jax.shard_map(
        per_device, mesh=mesh, in_specs=in_specs, out_specs=out_specs, check_vma=False
    )
```

```python
import functools

import jax
import jax.numpy as jnp
from jax import lax
from jax.experimental import pallas as pl
from jax.experimental.pallas import tpu as pltpu
from jax.sharding import PartitionSpec as P

base_step = 0.05
abs_tol = 0.01
rel_tol = 0.01
cores = 2
inner = 2
MESH = pl.DeviceIdType.MESH
f32 = jnp.float32
bf16 = jnp.bfloat16


def sigmoid(x):
    return 0.5 * jnp.tanh(0.5 * x) + 0.5


def dot(a, b):
    return jnp.dot(a, b, preferred_element_type=f32)


def dot_t(a, b):
    return lax.dot_general(a, b, (((1,), (1,)), ((), ())), preferred_element_type=f32)


def blocks(extent, width=256):
    width = min(width, extent)
    return [slice(at, at + width) for at in range(0, extent, width)]


def silu_pair(x):
    s = sigmoid(x)
    y = x * s
    return y.astype(bf16), s + y * (1.0 - s)


def prepare(ins, work):
    steps, rows = ins["mults"].shape
    table = work["table"]
    table[...] = jnp.zeros_like(table)
    table[0:steps, :] = ins["mults"][...].astype(f32) * base_step
    table[steps : 2 * steps, :] = ins["flags"][...].astype(f32)
    turned = table[...].T
    lanes = table.shape[0]
    for n in range(steps):
        h = jnp.broadcast_to(turned[:, n : n + 1], (rows, lanes))
        work["h"][n] = h
        work["r"][n] = jnp.sqrt(h)
        work["keep"][n] = jnp.broadcast_to(turned[:, steps + n : steps + n + 1], (rows, lanes))
    work["cur"][...] = ins["start"][...].astype(f32)
    work["cot"][...] = ins["cot"][...].astype(f32)
    work["err"][...] = jnp.zeros_like(work["err"])


late = ("w_up", "w_scale", "w_down", "noise")


def ready(n, ins, name):
    if "loads" in ins:

        @pl.when(n == 0)
        def _():
            ins["loads"][name].wait()


def forward(n, ins, work):
    rows, latent = work["cur"].shape
    hidden = ins["w_up"].shape[1]
    at = pl.ds(pl.multiple_of(n * rows, rows), rows)
    h = work["h"][n][:, 0:1]
    r = work["r"][n][:, 0:1]
    keep = work["keep"][n][:, 0:1]
    cur = work["cur"][...]
    low = cur.astype(bf16)
    work["low_t"][:, at] = cur.T.astype(bf16)
    for j in blocks(hidden):
        work["in1"][:, j], work["d_in1"][n, :, j] = silu_pair(dot(low, ins["w_spread"][:, j]))
    ready(n, ins, "w_up")
    for j in blocks(hidden):
        x = dot(low, ins["w_up"][:, j]) + ins["b_up"][:, j]
        work["hid"][at, j], work["d_hid"][n, :, j] = silu_pair(x)
    ready(n, ins, "w_scale")
    for j in blocks(latent):
        s = sigmoid(dot(work["in1"][...], ins["w_scale"][:, j]) + ins["b_scale"][:, j])
        g = 0.6 * s
        work["g"][:, j] = g
        work["d_g1"][n, :, j] = g * (1.0 - s)
        work["low2"][:, j] = (work["cur"][:, j] + g * r).astype(bf16)
    for j in blocks(hidden):
        work["in2"][:, j], work["d_in2"][n, :, j] = silu_pair(
            dot(work["low2"][...], ins["w_spread"][:, j])
        )
    ready(n, ins, "w_down")
    ready(n, ins, "noise")
    total = jnp.zeros((1, 128), f32)
    for j in blocks(latent):
        s = sigmoid(dot(work["in2"][...], ins["w_scale"][:, j]) + ins["b_scale"][:, j])
        gbar = 0.6 * s
        work["d_g2"][n, :, j] = gbar * (1.0 - s)
        drift = dot(work["hid"][at, :], ins["w_down"][:, j])
        noise = ins["noise"][n, :, j].astype(f32)
        g = work["g"][:, j]
        c = work["cur"][:, j]
        milstein = (gbar - g) * (0.5 * r * (noise * noise - 1.0))
        scaled = milstein / (abs_tol + rel_tol * jnp.abs(c))
        part = jnp.sum(scaled * scaled, axis=0, keepdims=True)
        for i in blocks(part.shape[1], 128):
            total = total + part[:, i]
        proposal = c + drift * h + g * (r * noise) + milstein
        work["cur"][:, j] = jnp.where(keep > 0.5, proposal, c)
    work["err"][pl.ds(n, 1), :] = total


def back_drift(n, ins, work):
    rows, latent = work["cur"].shape
    at = pl.ds(pl.multiple_of(n * rows, rows), rows)
    cd = work["cot"][...] * (work["keep"][n][:, 0:1] * work["h"][n][:, 0:1])
    work["cd"][...] = cd.astype(bf16)
    work["cd_t"][:, at] = cd.T.astype(bf16)


def back_pre(n, ins, work):
    rows, latent = work["cur"].shape
    hidden = ins["w_up"].shape[1]
    at = pl.ds(pl.multiple_of(n * rows, rows), rows)
    for j in blocks(hidden):
        back = dot_t(work["cd"][...], ins["w_down"][j, :])
        work["cpre"][at, j] = (back * work["d_hid"][n, :, j]).astype(bf16)


def back_state(n, ins, work):
    rows, latent = work["cur"].shape
    hidden = ins["w_up"].shape[1]
    at = pl.ds(pl.multiple_of(n * rows, rows), rows)
    r = work["r"][n][:, 0:1]
    keep = work["keep"][n][:, 0:1]
    for j in blocks(latent):
        noise = ins["noise"][n, :, j].astype(f32)
        ck = keep * work["cot"][:, j]
        to_bar = ck * (0.5 * r * (noise * noise - 1.0))
        work["to_g"][:, j] = ck * (r * noise) - to_bar
        work["d_out"][:, j] = (to_bar * work["d_g2"][n, :, j]).astype(bf16)
    for j in blocks(hidden):
        back = dot_t(work["d_out"][...], ins["w_scale"][j, :]).astype(bf16).astype(f32)
        work["in2"][:, j] = (back * work["d_in2"][n, :, j]).astype(bf16)
    for j in blocks(latent):
        back = dot_t(work["in2"][...], ins["w_spread"][j, :]).astype(bf16).astype(f32)
        work["g"][:, j] = back
        work["d_out"][:, j] = (
            (work["to_g"][:, j] + back * r) * work["d_g1"][n, :, j]
        ).astype(bf16)
    for j in blocks(hidden):
        back = dot_t(work["d_out"][...], ins["w_scale"][j, :]).astype(bf16).astype(f32)
        work["in1"][:, j] = (back * work["d_in1"][n, :, j]).astype(bf16)
    for j in blocks(latent):
        back = dot_t(work["in1"][...], ins["w_spread"][j, :]).astype(bf16).astype(f32)
        through = dot_t(work["cpre"][at, :], ins["w_up"][j, :])
        work["cot"][:, j] = work["cot"][:, j] + work["g"][:, j] + back + through


names = (
    "start", "w_up", "b_up", "w_down", "w_spread", "w_scale", "b_scale", "noise", "mults",
    "flags", "cot",
)


def work_shapes(steps, rows, latent, hidden):
    vm = pltpu.VMEM
    return dict(
        table=vm((128, rows), f32),
        h=vm((steps, rows, 128), f32),
        r=vm((steps, rows, 128), f32),
        keep=vm((steps, rows, 128), f32),
        cur=vm((rows, latent), f32),
        cot=vm((rows, latent), f32),
        err=vm((8, 128), f32),
        low_t=vm((latent, steps * rows), bf16),
        cd_t=vm((latent, steps * rows), bf16),
        hid=vm((steps * rows, hidden), bf16),
        cpre=vm((steps * rows, hidden), bf16),
        d_hid=vm((steps, rows, hidden), f32),
        in1=vm((rows, hidden), bf16),
        d_in1=vm((steps, rows, hidden), f32),
        in2=vm((rows, hidden), bf16),
        d_in2=vm((steps, rows, hidden), f32),
        g=vm((rows, latent), f32),
        d_g1=vm((steps, rows, latent), f32),
        d_g2=vm((steps, rows, latent), f32),
        low2=vm((rows, latent), bf16),
        cd=vm((rows, latent), bf16),
        to_g=vm((rows, latent), f32),
        d_out=vm((rows, latent), bf16),
    )


def local_kernel(work_names, *refs):
    ins = dict(zip(names, refs))
    err_ref, up_ref, down_ref = refs[len(names) : len(names) + 3]
    work = dict(zip(work_names, refs[len(names) + 3 :]))
    steps = ins["mults"].shape[0]
    prepare(ins, work)

    @pl.loop(0, steps)
    def _(n):
        forward(n, ins, work)

    err_ref[...] = work["err"][...]

    @pl.loop(0, steps - 1)
    def _(i):
        n = steps - 1 - i
        back_drift(n, ins, work)
        back_pre(n, ins, work)
        back_state(n, ins, work)

    back_drift(0, ins, work)
    back_pre(0, ins, work)
    for j in blocks(down_ref.shape[1]):
        down_ref[:, j] = dot(work["cd_t"][...], work["hid"][:, j])
        up_ref[:, j] = dot(work["low_t"][...], work["cpre"][:, j])


def whole_kernel(work_names, groups, members, total_count, *refs):
    ins = dict(zip(names, refs))
    err_ref, up_ref, down_ref = refs[len(names) : len(names) + 3]
    work = dict(zip(work_names, refs[len(names) + 3 :]))
    steps = ins["mults"].shape[0]
    latent, hidden = ins["w_up"].shape
    outer = members // (inner * cores)
    chunk = latent // members
    half = chunk // groups
    x = lax.axis_index("grp")
    place = lax.axis_index("dp")
    core = lax.rem(place, cores)
    y = lax.rem(place // cores, inner)
    z = place // (cores * inner)

    def at(g, o, i, c):
        return (g, (o * inner + i) * cores + c)

    mate = at(x, z, y, 1 - core)
    beside = at(x, z, 1 - y, core)
    across = at(1 - x, z, y, core)
    along = [at(x, lax.rem(z + 1 + k, outer), y, core) for k in range(outer - 1)]
    partners = [mate, beside, across] + along

    barrier = pltpu.get_barrier_semaphore()
    for partner in partners:
        pl.semaphore_signal(barrier, inc=1, device_id=partner, device_id_type=MESH)

    pending = {}

    def send(key, source, target, device):
        number = len(pending)
        pending[key] = pltpu.make_async_remote_copy(
            src_ref=source,
            dst_ref=target,
            send_sem=work["sent"].at[number],
            recv_sem=work["got"].at[number],
            device_id=device,
            device_id_type=MESH,
        )
        pending[key].start()

    loads = {}
    for i, name in enumerate(late):
        loads[name] = pltpu.make_async_copy(ins[name], work[name], work["loaded"].at[i])
        loads[name].start()
        ins[name] = work[name]
    ins["loads"] = loads
    prepare(ins, work)

    @pl.loop(0, steps)
    def _(n):
        forward(n, ins, work)

    pl.semaphore_wait(barrier, len(partners))
    err_in = work["err_in"]
    err_sum = work["err_sum"]
    send("e0", work["err"], err_in.at[0], mate)

    @pl.loop(0, steps - 1)
    def _(i):
        n = steps - 1 - i
        back_drift(n, ins, work)
        back_pre(n, ins, work)
        back_state(n, ins, work)

    pending["e0"].wait_recv()
    err_sum[0] = work["err"][...] + err_in[0]
    send("e1", err_sum.at[0], err_in.at[1], beside)
    back_drift(0, ins, work)

    grads = work["grads"]
    in0, in1, in2, in3, in4 = (work[f"arrive{i}"] for i in range(5))
    in1b = work["arrive1b"]
    mine = pl.ds(pl.multiple_of(x * half, half), half)
    other = pl.ds(pl.multiple_of((1 - x) * half, half), half)
    span = latent // outer

    def product(a, k):
        left, right = (("cd_t", "hid"), ("low_t", "cpre"))[a]
        piece = lax.rem(z + 1 + k, outer)
        rows = pl.ds(pl.multiple_of(piece * span, span), span)
        for j in blocks(hidden):
            value = dot(work[left][rows, :], work[right][:, j])
            grads[a, k, :, :, :, j] = value.reshape(inner, cores, chunk, value.shape[1])
        send((0, a, k), grads.at[a, k, :, 1 - core], in0.at[a, k], mate)

    def y_first(a, k):
        return (a == 0) if k == outer - 1 else (a + k) % 2 == 0

    def first(a, k):
        pending[0, a, k].wait_recv()
        grads[a, k, :, core] = grads[a, k, :, core] + in0[a, k]
        if y_first(a, k):
            send((1, a, k), grads.at[a, k, 1 - y, core], in1.at[a, k], beside)
        else:
            send((1, a, k), grads.at[a, k, :, core, other], in1b.at[a, k], across)

    def second(a, k):
        pending[1, a, k].wait_recv()
        if y_first(a, k):
            grads[a, k, y, core] = grads[a, k, y, core] + in1[a, k]
            send((2, a, k), grads.at[a, k, y, core, other], in2.at[a, k], across)
        else:
            grads[a, k, :, core, mine] = grads[a, k, :, core, mine] + in1b[a, k]
            send((2, a, k), grads.at[a, k, 1 - y, core, mine], in2.at[a, k], beside)

    def third(a, k):
        pending[2, a, k].wait_recv()
        grads[a, k, y, core, mine] = grads[a, k, y, core, mine] + in2[a, k]
        if k < outer - 1:
            send((3, a, k), grads.at[a, k, y, core, mine], in3.at[a, k], along[k])

    def fourth(a):
        value = grads[a, outer - 1, y, core, mine]
        for k in range(outer - 1):
            pending[3, a, k].wait_recv()
            value = value + in3[a, k]
        work["done"][a] = value
        send((4, a), work["done"].at[a], in4.at[a], across)
        (down_ref, up_ref)[a][mine, :] = value

    def fifth(a):
        pending[4, a].wait_recv()
        (down_ref, up_ref)[a][other, :] = in4[a]

    order = [(0, k) for k in range(outer - 1)] + [(1, k) for k in range(outer - 1)]
    order += [(0, outer - 1), (1, outer - 1)]
    for k in range(outer):
        product(0, k)
    first(*order[0])
    first(*order[1])
    back_pre(0, ins, work)
    for k in range(outer):
        product(1, k)
    pending["e1"].wait_recv()
    err_sum[1] = err_sum[0] + err_in[1]
    send("e2", err_sum.at[1], err_in.at[2], across)
    count = len(order)
    for at_pair in range(2, count + 4, 2):
        for i in (at_pair, at_pair + 1):
            if i < count:
                first(*order[i])
        for i in (at_pair - 2, at_pair - 1):
            if i < count:
                second(*order[i])
        for i in (at_pair - 4, at_pair - 3):
            if 0 <= i < count:
                third(*order[i])
        if at_pair == 4:
            pending["e2"].wait_recv()
            err_sum[2] = err_sum[1] + err_in[2]
            for i in range(outer - 1):
                send(("e3", i), err_sum.at[2], err_in.at[3 + i], along[i])
    fourth(0)
    fourth(1)
    total = err_sum[2]
    for i in range(outer - 1):
        pending["e3", i].wait_recv()
        total = total + err_in[3 + i]
    norms = jnp.sqrt(jnp.sum(total, axis=1, keepdims=True) * (1.0 / total_count))
    for n in range(steps):
        err_ref[n] = jnp.sum(norms[n : n + 1, 0:1])
    fifth(0)
    fifth(1)
    for copy in pending.values():
        copy.wait_send()


def hand_over(err_ref, up_ref, down_ref, err_out, up_out, down_out):
    up_out[...] = up_ref[...]
    down_out[...] = down_ref[...]
    for n in range(err_out.shape[0]):
        err_out[n] = err_ref[n]


def per_device(
    start_state, w_up, b_up, w_down, w_spread, w_scale, b_scale, brownian_noise, step_mults,
    accept_flags, cotangent,
):
    groups = lax.axis_size("grp")
    members = lax.axis_size("dp")
    rows, latent = start_state.shape
    hidden = w_up.shape[1]
    steps = brownian_noise.shape[0]
    total_count = rows * latent * groups * members
    args = (
        start_state, w_up, b_up[None, :], w_down, w_spread, w_scale, b_scale[None, :],
        brownian_noise, step_mults, accept_flags, cotangent,
    )
    work = work_shapes(steps, rows, latent, hidden)
    vmem = pl.BlockSpec(memory_space=pltpu.VMEM)
    chunk = latent // members
    paired = groups == 2 and members % (inner * cores) == 0 and members > inner * cores
    if not paired or chunk % (8 * groups) != 0:
        err, up, down = pl.pallas_call(
            functools.partial(local_kernel, tuple(work)),
            out_shape=(
                jax.ShapeDtypeStruct((8, 128), f32),
                jax.ShapeDtypeStruct((latent, hidden), f32),
                jax.ShapeDtypeStruct((latent, hidden), f32),
            ),
            in_specs=[vmem] * len(args),
            out_specs=(vmem,) * 3,
            scratch_shapes=list(work.values()),
            compiler_params=pltpu.CompilerParams(vmem_limit_bytes=56 * 2**20),
        )(*args)
        totals = lax.psum(jnp.sum(err[:steps], axis=1), ("grp", "dp"))
        up, down = (
            lax.psum_scatter(g, "dp", scatter_dimension=0, tiled=True) for g in (up, down)
        )
        up, down = lax.psum((up, down), "grp")
        return (jnp.sqrt(totals / total_count), up, down)
    outer = members // (inner * cores)
    half = chunk // groups
    vm = pltpu.VMEM
    copies = 6 * outer + 2 * (outer - 1) + 2 + 3 + outer - 1
    work.update(
        grads=vm((2, outer, inner, cores, chunk, hidden), f32),
        arrive0=vm((2, outer, inner, chunk, hidden), f32),
        arrive1=vm((2, outer, chunk, hidden), f32),
        arrive1b=vm((2, outer, inner, half, hidden), f32),
        arrive2=vm((2, outer, half, hidden), f32),
        arrive3=vm((2, outer - 1, half, hidden), f32),
        arrive4=vm((2, half, hidden), f32),
        done=vm((2, half, hidden), f32),
        err_in=vm((2 + outer, 8, 128), f32),
        err_sum=vm((3, 8, 128), f32),
        sent=pltpu.SemaphoreType.DMA((copies,)),
        got=pltpu.SemaphoreType.DMA((copies,)),
        loaded=pltpu.SemaphoreType.DMA((len(late),)),
        w_up=vm(w_up.shape, bf16),
        w_scale=vm(w_scale.shape, bf16),
        w_down=vm(w_down.shape, bf16),
        noise=vm(brownian_noise.shape, bf16),
    )
    out_shape = (
        jax.ShapeDtypeStruct((steps,), f32),
        jax.ShapeDtypeStruct((chunk, hidden), f32),
        jax.ShapeDtypeStruct((chunk, hidden), f32),
    )
    results = pl.pallas_call(
        functools.partial(whole_kernel, tuple(work), groups, members, total_count),
        out_shape=out_shape,
        in_specs=[pl.BlockSpec(memory_space=pl.ANY) if name in late else vmem for name in names],
        out_specs=(pl.BlockSpec(memory_space=pltpu.SMEM), vmem, vmem),
        scratch_shapes=list(work.values()),
        compiler_params=pltpu.CompilerParams(
            vmem_limit_bytes=56 * 2**20, collective_id=0, has_side_effects=True
        ),
    )(*args)
    smem = pl.BlockSpec(memory_space=pltpu.SMEM)
    return pl.pallas_call(
        hand_over,
        out_shape=out_shape,
        in_specs=[smem, vmem, vmem],
        out_specs=(smem, vmem, vmem),
        compiler_params=pltpu.CompilerParams(vmem_limit_bytes=60 * 2**20),
    )(*results)


def solution(mesh):
    in_specs = (
        P(("grp", "dp"), None),
        P(),
        P(),
        P(),
        P(),
        P(),
        P(),
        P(None, ("grp", "dp"), None),
        P(None, ("grp", "dp")),
        P(None, ("grp", "dp")),
        P(("grp", "dp"), None),
    )
    out_specs = (P(), P("dp", None), P("dp", None))
    return jax.shard_map(
        per_device, mesh=mesh, in_specs=in_specs, out_specs=out_specs, check_vma=False
    )
```
